1024 devices in a mesh: grp: 8 (over x, core), nbr: 128 (over z, y).
Axes of the slice: x: 4, y: 4, z: 32, core: 2. Of those that a mesh axis runs over, the one named last changes fastest.
Arguments:
- multipole: bfloat16 [488, 262144], P(None, ('grp', 'nbr')), may hold values from -6 to 6
- dest: int32 [262144, 1], P(('grp', 'nbr')), may hold values from 0 to 7; in each aligned block of 256 rows (0 to 255, 256 to 511, ...) at most 64 rows name the same one
- parent_local: bfloat16 [488, 32768], P(None, ('grp', 'nbr')), may hold values from -6 to 6
- parent_of: int32 [524288], P(('grp', 'nbr')), may hold values from 0 to 255
- send_list: int32 [2, 262144], P(None, ('grp', 'nbr')), may hold values from 0 to 511, as said below
- lists: int32 [8, 524288], P(None, ('grp', 'nbr')), may hold values from -1 to 1023, as said below
- m2l_ops: bfloat16 [8, 488, 488], replicated, may hold values from -0.25 to 0.25
- l2l_ops: bfloat16 [8, 488, 488], replicated, may hold values from -0.25 to 0.25
Outputs:
- local_exp: float32 [488, 524288], P(None, ('grp', 'nbr'))
The draws below stay inside these ranges and needn't reach their ends.
Inputs may be any that keep to these rules, and one draw needn't show every extreme that they name: `dest`: no leaf owner sends more than 64 boxes to one owner, and some leaf owner sends exactly 64. `send_list`: each owner's two rows together list each of its 512 slots once. `lists`: -1 marks padding.
All inputs are finite; a program needn't handle non-finite values.
Results may differ from the reference program's by a relative error of at most 0.0003.
Values may be sent and summed in bfloat16 or wider, within the bound.
A program may use at most 32 MiB of HBM per device.

```python
import math
import jax
import jax.numpy as jnp
import numpy as np

COEF = 488
OFFSETS = 8
BOX_DEV = 256
CAP = 64
SLOTS = 512
RIM = 256
PARENTS_DEV = 32
BOXES = 262144
ALL_SLOTS = 524288
ALL_RIM = 262144
ALL_PAR = 32768
N_GRP = 8
N_NBR = 128


def draw_send_list(key, part):
    key = jax.random.fold_in(key, 3)
    dev_count = ALL_SLOTS // SLOTS
    subkeys = jax.random.split(key, dev_count)
    shuffled = jax.vmap(lambda subkey: jax.random.permutation(subkey, SLOTS))(subkeys)
    return shuffled.reshape(dev_count, 2, RIM).transpose(1, 0, 2).reshape(2, ALL_RIM).astype(jnp.int32)


def draw_lists(key, part):
    key = jax.random.fold_in(key, 5)
    key_kind, key_own, key_pick = jax.random.split(key, 3)
    category = jax.random.randint(key_kind, (OFFSETS, ALL_SLOTS), 0, 4)
    own_slot = jax.random.randint(key_own, (OFFSETS, ALL_SLOTS), 0, SLOTS)
    rim_pick = jax.random.randint(key_pick, (OFFSETS, ALL_SLOTS), 0, RIM)
    picked = jnp.where(category == 2, SLOTS + rim_pick, SLOTS + RIM + rim_pick)
    picked = jnp.where(category == 1, own_slot, picked)
    picked = jnp.where(category == 0, -1, picked)
    return picked.astype(jnp.int32)


def place_ends(values, stream_key, smallest, largest):
    place = [jax.random.randint(jax.random.fold_in(stream_key, axis), (), 0, length) for axis, length in enumerate(values.shape)]
    widest = values.shape.index(max(values.shape))
    beside = place[:widest] + [(place[widest] + 1) % values.shape[widest]] + place[widest + 1:]
    return values.at[tuple(place)].set(smallest).at[tuple(beside)].set(largest)


def shard_levels(own_key, dims, cuts, least, largest):
    def one(dim, shards_of):
        heights = jax.random.uniform(jax.random.fold_in(jax.random.fold_in(own_key, 6), dim), (shards_of,), jnp.float32, least / len(cuts), largest / len(cuts))
        return jnp.repeat(jnp.exp(heights), dims[dim] // shards_of).reshape((-1,) + (1,) * (len(dims) - dim - 1))

    level = one(*cuts[0])
    for cut in cuts[1:]:
        level = level * one(*cut)
    return level


def assign_block(stream_key, own, number, rows, amount, top, reach, slope):
    order = jax.random.permutation(stream_key, amount)
    packed, common = load_shares(amount, rows * top, reach, slope, True), load_shares(amount, rows * top, reach, slope, False)
    places = jnp.arange(amount)

    def named(lengths, turn):
        used = int((lengths > 0).sum())
        fixed = max(1, used // 4)
        shifted = fixed + (places - fixed + turn * (used - fixed)) % max(1, amount - fixed)
        return jnp.zeros((amount,), jnp.int32).at[order[jnp.where(places < fixed, places, shifted)]].set(jnp.asarray(lengths, jnp.int32))

    lengths = jnp.where(number % 4 == 0, named(packed, number // 4), named(common, number - number // 4 - 1))
    mixed = jax.random.permutation(jax.random.fold_in(own, 3), amount)
    source_of, receiver = mixed[0:amount // 2 * 2:2], mixed[1:amount // 2 * 2:2]
    room = jnp.minimum(lengths[source_of] - 1, reach - lengths[receiver]) // 2
    room = jnp.where((source_of == order[0]) | (receiver == order[0]) | (lengths[receiver] == 0), 0, jnp.maximum(room, 0))
    shifted = jax.random.randint(jax.random.fold_in(own, 4), (amount // 2,), 0, 1 << 20) % (room + 1)
    lengths = lengths.at[source_of].add(-shifted).at[receiver].add(shifted)
    labels = jnp.searchsorted(jnp.cumsum(lengths), jnp.arange(rows * top), side="right").astype(jnp.int32)
    grid = labels.reshape(top, rows).T
    grid = grid[jax.random.permutation(jax.random.fold_in(own, 1), rows)]
    turn = jax.random.randint(jax.random.fold_in(own, 2), (rows, 1), 0, top)
    return jnp.take_along_axis(grid, (jnp.arange(top)[None, :] + turn) % top, axis=1)


def load_shares(number_of, total, reach, slope, full):
    loads = [(1 << 20) // math.isqrt(standing ** slope) + 1 for standing in range(1, number_of + 1)]
    largest = reach if full else min(reach, max(-(-total // number_of), total * loads[0] // sum(loads)))
    least = 1 if total - largest >= number_of - 1 else 0
    holding, spare = [largest] + [least] * (number_of - 1), total - largest - least * (number_of - 1)
    while spare > 0:
        free = [i for i in range(1, number_of) if holding[i] < largest] or [i for i in range(1, number_of) if holding[i] < reach]
        mass, left = sum([loads[i] for i in free]), spare
        for i in free:
            addition = min(reach - holding[i], max(1, left * loads[i] // mass), spare)
            holding[i] = holding[i] + addition
            spare = spare - addition
    return np.array(holding)


def bell_draw(key, dims, deviation, most, cuts=(), held_as=jnp.bfloat16):
    values = deviation * jax.random.normal(key, dims, jnp.float32)
    if cuts:
        values = values * shard_levels(key, dims, cuts, -0.22, 0.18)
    return jnp.clip(values, -most, most).astype(held_as)


def setup_inputs(seed: int = 0) -> dict:
    key_list = jax.random.split(jax.random.key(seed), 9)
    multipole = bell_draw(key_list[0], (COEF, BOXES), 1.0, 6.0, ((1, 1024),))
    dest_keys = jax.random.split(jax.random.fold_in(key_list[1], 1), BOXES // BOX_DEV)
    dest_turns = jax.random.permutation(jax.random.fold_in(key_list[1], 3), BOXES // BOX_DEV)
    dest = jax.vmap(lambda own, number: assign_block(jax.random.fold_in(key_list[1], 2), own, number, BOX_DEV, N_GRP, 1, CAP, 2))(dest_keys, dest_turns).reshape((BOXES, 1))
    parent_local = bell_draw(key_list[2], (COEF, ALL_PAR), 1.0, 6.0, ((1, 1024),))
    parent_of = place_ends(jax.random.randint(key_list[3], (ALL_SLOTS,), 0, BOX_DEV), jax.random.fold_in(key_list[3], 1), 0, BOX_DEV - 1).astype(jnp.int32)
    send_list = draw_send_list(jax.random.fold_in(key_list[8], 71), 0)
    lists = draw_lists(jax.random.fold_in(key_list[8], 71), 0)
    m2l_ops = bell_draw(key_list[6], (OFFSETS, COEF, COEF), COEF ** -0.5, 0.25)
    l2l_ops = bell_draw(key_list[7], (8, COEF, COEF), COEF ** -0.5, 0.25)
    return {"multipole": multipole, "dest": dest, "parent_local": parent_local, "parent_of": parent_of, "send_list": send_list, "lists": lists, "m2l_ops": m2l_ops, "l2l_ops": l2l_ops}


def relay_boxes(multipole, dest):
    dev_count = N_GRP * N_NBR
    target = dest[:, 0].reshape(dev_count, BOX_DEV)
    onehot = (target[:, :, None] == jnp.arange(N_GRP, dtype=jnp.int32)[None, None, :]).astype(jnp.int32)
    arrival = jnp.sum((jnp.cumsum(onehot, axis=1) - 1) * onehot, axis=2)
    device_of = jnp.arange(dev_count, dtype=jnp.int32)[:, None]
    group_of = device_of // N_NBR
    column_of = device_of % N_NBR
    landing = ((target * N_NBR + column_of) * N_GRP + group_of) * CAP + arrival
    return jnp.zeros((COEF, ALL_SLOTS), jnp.bfloat16).at[:, landing.reshape(-1)].set(multipole)


def reference(multipole, dest, parent_local, parent_of, send_list, lists, m2l_ops, l2l_ops):
    dev_count = N_GRP * N_NBR
    owned_coef = relay_boxes(multipole, dest)
    slot_index = jnp.arange(ALL_SLOTS, dtype=jnp.int32)
    device_of = slot_index // SLOTS
    column_of = device_of % N_NBR
    translated = jnp.stack([jnp.dot(l2l_ops[octant], parent_local, preferred_element_type=jnp.float32) for octant in range(8)])
    translated = translated.transpose(1, 0, 2).reshape(COEF, 8 * ALL_PAR)
    octant_of = parent_of // PARENTS_DEV
    parent_col = device_of * PARENTS_DEV + parent_of % PARENTS_DEV
    accum_local = jnp.take(translated, octant_of * ALL_PAR + parent_col, axis=1)
    left_dev = jnp.clip(device_of - 1, 0, dev_count - 1)
    right_dev = jnp.clip(device_of + 1, 0, dev_count - 1)
    for offset in range(OFFSETS):
        entries = lists[offset]
        is_own = (entries >= 0) & (entries < SLOTS)
        is_left = (entries >= SLOTS) & (entries < SLOTS + RIM)
        is_right = entries >= SLOTS + RIM
        left_pick = jnp.clip(entries - SLOTS, 0, RIM - 1)
        right_pick = jnp.clip(entries - SLOTS - RIM, 0, RIM - 1)
        left_slot = send_list[0, left_dev * RIM + left_pick]
        right_slot = send_list[1, right_dev * RIM + right_pick]
        source_col = jnp.where(is_own, device_of * SLOTS + jnp.clip(entries, 0, SLOTS - 1),
                               jnp.where(is_left, left_dev * SLOTS + left_slot, right_dev * SLOTS + right_slot))
        usable = is_own | (is_left & (column_of > 0)) | (is_right & (column_of < N_NBR - 1))
        columns = jnp.take(owned_coef, source_col, axis=1)
        columns = jnp.where(usable[None, :], columns, jnp.zeros_like(columns))
        accum_local = accum_local + jnp.dot(m2l_ops[offset], columns, preferred_element_type=jnp.float32)
    return accum_local
```

```python
import functools

import jax
import jax.numpy as jnp
from jax import lax
from jax.experimental import pallas as pl
from jax.experimental.pallas import tpu as pltpu
from jax.sharding import PartitionSpec as P

MESH = pl.DeviceIdType.MESH
LANES = 128
F32 = jnp.float32
BF16 = jnp.bfloat16


def nt_dot(a, b):
    return lax.dot_general(a, b, (((1,), (1,)), ((), ())), preferred_element_type=F32)


def nn_dot(a, b):
    return jnp.dot(a, b, preferred_element_type=F32)


def iota(shape, dim):
    return lax.broadcasted_iota(jnp.int32, shape, dim)


def as_bf16(mask):
    return jnp.where(mask, jnp.ones((), F32), jnp.zeros((), F32)).astype(BF16)


def down_columns(row):
    return jnp.transpose(jnp.broadcast_to(row, (LANES, row.shape[1])))


def kernel(
    groups, columns, coef, boxes, slots, rim, parents, offsets, octants, chunks,
    mult_hbm, dest_hbm, par_hbm, pof_hbm, send_hbm, list_hbm, m2l_hbm, l2l_hbm,
    out_ref,
    mult, dest, par, pof, send, entries, m2l, l2l,
    outgoing, own, offer, near, hot, cols, blocks,
    in_sem, a_send, a_recv, n_send, n_recv,
):
    cap = slots // groups
    halves = chunks // 2
    g = lax.axis_index("grp")
    n = lax.axis_index("nbr")
    after = lax.rem(n + 1, columns)
    before = lax.rem(n + columns - 1, columns)

    loads = [
        pltpu.make_async_copy(src, dst, in_sem.at[i])
        for i, (src, dst) in enumerate(
            (
                (dest_hbm, dest),
                (mult_hbm, mult),
                (send_hbm, send),
                (list_hbm, entries),
                (par_hbm, par),
                (pof_hbm, pof),
                (l2l_hbm, l2l),
                (m2l_hbm, m2l),
            )
        )
    ]
    for load in loads:
        load.start()

    barrier = pltpu.get_barrier_semaphore()
    for d in range(1, groups):
        pl.semaphore_signal(
            barrier, inc=1, device_id=(lax.rem(g + d, groups), n), device_id_type=MESH
        )
    for to in (after, before):
        pl.semaphore_signal(barrier, inc=1, device_id=(g, to), device_id_type=MESH)

    loads[0].wait()
    owner = dest[...]
    named = iota((groups, boxes), 0) == owner
    earlier = as_bf16(iota((boxes, boxes), 0) < iota((boxes, boxes), 1))
    counts = nn_dot(as_bf16(named), earlier)
    arrival = jnp.sum(jnp.where(named, counts, jnp.zeros_like(counts)), axis=0, keepdims=True)
    position = owner * cap + arrival.astype(jnp.int32)
    placing = as_bf16(iota((slots, boxes), 0) == position)

    outgoing[chunks - 1] = jnp.zeros((slots, LANES), BF16)
    loads[1].wait()
    placed = nt_dot(placing, mult[...]).astype(BF16)
    for c in range(chunks):
        width = min(LANES, coef - c * LANES)
        outgoing[c, :, :width] = placed[:, c * LANES : c * LANES + width]
    mine = pl.ds(pl.multiple_of(g * cap, cap), cap)
    for c in range(chunks):
        own[c, mine, :] = outgoing[c, mine, :]

    def relay(c, d):
        to = lax.rem(g + d, groups)
        return pltpu.make_async_remote_copy(
            src_ref=outgoing.at[c, pl.ds(pl.multiple_of(to * cap, cap), cap)],
            dst_ref=own.at[c, mine],
            send_sem=a_send.at[c, d - 1],
            recv_sem=a_recv.at[c, d - 1],
            device_id=(to, n),
            device_id_type=MESH,
        )

    def hand(c, side):
        return pltpu.make_async_remote_copy(
            src_ref=offer.at[c, pl.ds(side * rim, rim)],
            dst_ref=near.at[c, pl.ds(side * rim, rim)],
            send_sem=n_send.at[c, side],
            recv_sem=n_recv.at[c, side],
            device_id=(g, (after, before)[side]),
            device_id_type=MESH,
        )

    pl.semaphore_wait(barrier, groups + 1)
    for c in range(chunks):
        for d in range(1, groups):
            relay(c, d).start()

    loads[2].wait()
    lane = iota((rim, LANES), 1)
    picks = []
    for side in range(2):
        wanted = down_columns(send[side : side + 1, :])
        picks.append(
            jnp.concatenate(
                [as_bf16(wanted == lane + t * LANES) for t in range(slots // LANES)], axis=1
            )
        )
    pick = jnp.concatenate(picks, axis=0)

    loads[3].wait()
    listed = entries[...]
    from_left = (listed >= slots) & (listed < slots + rim)
    from_right = listed >= slots + rim
    listed = jnp.where(from_left & (n == 0), -1, listed)
    entries[...] = jnp.where(from_right & (n == columns - 1), -1, listed)
    slot_lane = iota((slots, LANES), 1)

    def build(k):
        wanted = down_columns(entries[k : k + 1, :])
        for t in range(hot.shape[2] // LANES):
            hot[k, :, t * LANES : (t + 1) * LANES] = as_bf16(wanted == slot_lane + t * LANES)

    def pass_on(c):
        for d in range(1, groups):
            relay(c, d).wait_recv()
        offer[c] = nn_dot(pick, own[c]).astype(BF16)
        for side in range(2):
            hand(c, side).start()

    for k in range(offsets // 2):
        build(k)
    pass_on(0)
    for k in range(offsets // 2, offsets):
        build(k)
    pass_on(1)

    for i in (4, 5, 6):
        loads[i].wait()
    blocks[...] = jnp.zeros(blocks.shape, BF16)
    for q in range(octants):
        blocks[q, pl.ds(q * parents, parents), :] = par[...]
    translated = nt_dot(l2l[0], blocks[0])
    for q in range(1, octants):
        translated = translated + nt_dot(l2l[q], blocks[q])
    pass_on(2)
    upper = translated.astype(BF16)
    lower = (translated - upper.astype(F32)).astype(BF16)
    child = as_bf16(iota((octants * parents, slots), 0) == pof[...])
    out_ref[...] = nn_dot(upper, child) + nn_dot(lower, child)
    pass_on(3)

    def half_of(ref, h):
        return jnp.concatenate([ref[2 * h], ref[2 * h + 1]], axis=1)

    for h in range(halves):
        local = half_of(own, h)
        for k in range(offsets):
            cols[h, k] = nn_dot(hot[k, :, :slots], local).astype(BF16)

    loads[7].wait()
    for h in range(halves):
        for c in (2 * h, 2 * h + 1):
            for side in range(2):
                hand(c, side).wait_recv()
        beside = half_of(near, h)
        for k in range(offsets):
            cols[h, k] = cols[h, k] + nn_dot(hot[k, :, slots:], beside).astype(BF16)
        first = h * 2 * LANES
        width = min(2 * LANES, coef - first)
        total = out_ref[...]
        for k in range(offsets):
            total = total + nt_dot(m2l[k, :, first : first + width], cols[h, k, :, :width])
        out_ref[...] = total

    for c in range(chunks):
        for d in range(1, groups):
            relay(c, d).wait_send()
        for side in range(2):
            hand(c, side).wait_send()


def body(multipole, dest, parent_local, parent_of, send_list, lists, m2l_ops, l2l_ops):
    groups, columns = lax.axis_size("grp"), lax.axis_size("nbr")
    coef, boxes = multipole.shape
    offsets, slots = lists.shape
    octants = l2l_ops.shape[0]
    rim = send_list.shape[1]
    parents = parent_local.shape[1]
    chunks = -(-coef // LANES)
    dest_row = dest.reshape(1, boxes)
    parent_rows = parent_local.T
    child_row = parent_of.reshape(1, slots)
    args = (multipole, dest_row, parent_rows, child_row, send_list, lists, m2l_ops, l2l_ops)
    return pl.pallas_call(
        functools.partial(
            kernel, groups, columns, coef, boxes, slots, rim, parents, offsets, octants, chunks
        ),
        out_shape=jax.ShapeDtypeStruct((coef, slots), F32),
        in_specs=[pl.BlockSpec(memory_space=pl.ANY)] * len(args),
        out_specs=pl.BlockSpec(memory_space=pltpu.VMEM),
        scratch_shapes=[pltpu.VMEM(a.shape, a.dtype) for a in args]
        + [
            pltpu.VMEM((chunks, slots, LANES), BF16),
            pltpu.VMEM((chunks, slots, LANES), BF16),
            pltpu.VMEM((chunks, 2 * rim, LANES), BF16),
            pltpu.VMEM((chunks, 2 * rim, LANES), BF16),
            pltpu.VMEM((offsets, slots, slots + 2 * rim), BF16),
            pltpu.VMEM((chunks // 2, offsets, slots, 2 * LANES), BF16),
            pltpu.VMEM((octants, octants * parents, coef), BF16),
            pltpu.SemaphoreType.DMA((len(args),)),
            pltpu.SemaphoreType.DMA((chunks, groups - 1)),
            pltpu.SemaphoreType.DMA((chunks, groups - 1)),
            pltpu.SemaphoreType.DMA((chunks, 2)),
            pltpu.SemaphoreType.DMA((chunks, 2)),
        ],
        compiler_params=pltpu.CompilerParams(
            collective_id=0, has_side_effects=True, vmem_limit_bytes=48 * 1024 * 1024
        ),
        name="downward",
    )(*args)


def solution(mesh):
    placed = (
        P(None, ("grp", "nbr")),
        P(("grp", "nbr"), None),
        P(None, ("grp", "nbr")),
        P(("grp", "nbr")),
        P(None, ("grp", "nbr")),
        P(None, ("grp", "nbr")),
        P(),
        P(),
    )
    return jax.shard_map(
        body, mesh=mesh, in_specs=placed, out_specs=P(None, ("grp", "nbr")), check_vma=False
    )
```

```python
import functools

import jax
import jax.numpy as jnp
from jax import lax
from jax.experimental import pallas as pl
from jax.experimental.pallas import tpu as pltpu
from jax.sharding import PartitionSpec as P

MESH = pl.DeviceIdType.MESH
LANES = 128
F32 = jnp.float32
BF16 = jnp.bfloat16


def nt_dot(a, b):
    return lax.dot_general(a, b, (((1,), (1,)), ((), ())), preferred_element_type=F32)


def nn_dot(a, b):
    return jnp.dot(a, b, preferred_element_type=F32)


def iota(shape, dim):
    return lax.broadcasted_iota(jnp.int32, shape, dim)


def as_bf16(mask):
    return jnp.where(mask, jnp.ones((), F32), jnp.zeros((), F32)).astype(BF16)


def down_columns(row):
    return jnp.transpose(jnp.broadcast_to(row, (LANES, row.shape[1])))


def kernel(
    groups, columns, coef, boxes, slots, rim, parents, offsets, octants, chunks,
    mult_hbm, dest_hbm, par_hbm, pof_hbm, send_hbm, list_hbm, m2l_hbm, l2l_hbm,
    out_ref,
    mult, dest, par, pof, send, entries, m2l, l2l,
    outgoing, own, offer, near, hot, cols, blocks,
    in_sem, a_send, a_recv, n_send, n_recv, group_in, columns_in,
):
    cap = slots // groups
    halves = chunks // 2
    g = lax.axis_index("grp")
    n = lax.axis_index("nbr")
    after, before = n + 1, n - 1
    has_after, has_before = n < columns - 1, n > 0

    loads = [
        pltpu.make_async_copy(src, dst, in_sem.at[i])
        for i, (src, dst) in enumerate(
            (
                (dest_hbm, dest),
                (mult_hbm, mult),
                (send_hbm, send),
                (list_hbm, entries),
                (par_hbm, par),
                (pof_hbm, pof),
                (l2l_hbm, l2l),
                (m2l_hbm, m2l),
            )
        )
    ]
    for load in loads:
        load.start()

    barrier = pltpu.get_barrier_semaphore()

    def tell(semaphore, member, column):
        pl.semaphore_signal(semaphore, inc=1, device_id=(member, column), device_id_type=MESH)

    @pl.when(g > 0)
    def _():
        tell(barrier, 0, n)

    for has, to in ((has_after, after), (has_before, before)):

        @pl.when(has)
        def _():
            tell(barrier, jnp.maximum(g, 1), to)

    loads[0].wait()
    owner = dest[...]
    named = iota((groups, boxes), 0) == owner
    earlier = as_bf16(iota((boxes, boxes), 0) < iota((boxes, boxes), 1))
    counts = nn_dot(as_bf16(named), earlier)
    arrival = jnp.sum(jnp.where(named, counts, jnp.zeros_like(counts)), axis=0, keepdims=True)
    position = owner * cap + arrival.astype(jnp.int32)
    placing = as_bf16(iota((slots, boxes), 0) == position)

    outgoing[chunks - 1] = jnp.zeros((slots, LANES), BF16)
    loads[1].wait()
    placed = nt_dot(placing, mult[...]).astype(BF16)
    for c in range(chunks):
        width = min(LANES, coef - c * LANES)
        outgoing[c, :, :width] = placed[:, c * LANES : c * LANES + width]
    mine = pl.ds(pl.multiple_of(g * cap, cap), cap)
    for c in range(chunks):
        own[c, mine, :] = outgoing[c, mine, :]

    def relay(c, d):
        to = lax.rem(g + d, groups)
        return pltpu.make_async_remote_copy(
            src_ref=outgoing.at[c, pl.ds(pl.multiple_of(to * cap, cap), cap)],
            dst_ref=own.at[c, mine],
            send_sem=a_send.at[c, d - 1],
            recv_sem=a_recv.at[c, d - 1],
            device_id=(to, n),
            device_id_type=MESH,
        )

    def hand(c, side):
        return pltpu.make_async_remote_copy(
            src_ref=offer.at[c, pl.ds(side * rim, rim)],
            dst_ref=near.at[c, pl.ds(side * rim, rim)],
            send_sem=n_send.at[c, side],
            recv_sem=n_recv.at[c, side],
            device_id=(g, (after, before)[side]),
            device_id_type=MESH,
        )

    @pl.when(g == 0)
    def _():
        pl.semaphore_wait(barrier, groups - 1)
        for member in range(1, groups):
            tell(group_in, member, n)

    @pl.when(g > 0)
    def _():
        pl.semaphore_wait(group_in, 1)

    for c in range(chunks):
        for d in range(1, groups):
            relay(c, d).start()

    loads[2].wait()
    lane = iota((rim, LANES), 1)
    picks = []
    for side in range(2):
        wanted = down_columns(send[side : side + 1, :])
        picks.append(
            jnp.concatenate(
                [as_bf16(wanted == lane + t * LANES) for t in range(slots // LANES)], axis=1
            )
        )
    pick = jnp.concatenate(picks, axis=0)

    loads[3].wait()
    listed = entries[...]
    from_left = (listed >= slots) & (listed < slots + rim)
    from_right = listed >= slots + rim
    listed = jnp.where(from_left & (n == 0), -1, listed)
    entries[...] = jnp.where(from_right & (n == columns - 1), -1, listed)
    slot_lane = iota((slots, LANES), 1)

    def build(k):
        wanted = down_columns(entries[k : k + 1, :])
        for t in range(hot.shape[2] // LANES):
            hot[k, :, t * LANES : (t + 1) * LANES] = as_bf16(wanted == slot_lane + t * LANES)

    def know_columns():
        ends = columns - 1
        beside = (n + ends) // columns + (ends - n + ends) // columns

        @pl.when(g > 1)
        def _():
            pl.semaphore_wait(barrier, beside)

        @pl.when(g == 1)
        def _():
            pl.semaphore_wait(barrier, 2 * beside)

        @pl.when(g == 1)
        def _():
            tell(columns_in, 0, n)

        @pl.when(g == 0)
        def _():
            pl.semaphore_wait(columns_in, 1)

    def pass_on(c):
        for d in range(1, groups):
            relay(c, d).wait_recv()
        offer[c] = nn_dot(pick, own[c]).astype(BF16)
        if c == 0:
            know_columns()
        for side, has in enumerate((has_after, has_before)):

            @pl.when(has)
            def _():
                hand(c, side).start()

    def half_of(ref, h):
        return jnp.concatenate([ref[2 * h], ref[2 * h + 1]], axis=1)

    def from_own(h):
        local = half_of(own, h)
        for k in range(offsets):
            cols[h, k] = nn_dot(hot[k, :, :slots], local).astype(BF16)

    for k in range(offsets):
        build(k)

    for i in (4, 5, 6):
        loads[i].wait()
    blocks[...] = jnp.zeros(blocks.shape, BF16)
    for q in range(octants):
        blocks[q, pl.ds(q * parents, parents), :] = par[...]
    translated = nt_dot(l2l[0], blocks[0])
    for q in range(1, octants // 2):
        translated = translated + nt_dot(l2l[q], blocks[q])
    out_ref[:, : octants * parents] = translated
    pass_on(0)
    translated = out_ref[:, : octants * parents]
    for q in range(octants // 2, octants):
        translated = translated + nt_dot(l2l[q], blocks[q])
    upper = translated.astype(BF16)
    lower = (translated - upper.astype(F32)).astype(BF16)
    child = as_bf16(iota((octants * parents, slots), 0) == pof[...])
    out_ref[...] = nn_dot(upper, child) + nn_dot(lower, child)
    pass_on(1)
    from_own(0)
    pass_on(2)
    pass_on(3)
    for h in range(1, halves):
        from_own(h)

    @pl.when(n == 0)
    def _():
        near[:, :rim] = jnp.zeros((chunks, rim, LANES), BF16)

    @pl.when(n == columns - 1)
    def _():
        near[:, rim:] = jnp.zeros((chunks, rim, LANES), BF16)

    loads[7].wait()
    for h in range(halves):
        for c in (2 * h, 2 * h + 1):
            for side, has in enumerate((has_before, has_after)):

                @pl.when(has)
                def _():
                    hand(c, side).wait_recv()

        beside = half_of(near, h)
        for k in range(offsets):
            cols[h, k] = cols[h, k] + nn_dot(hot[k, :, slots:], beside).astype(BF16)
        first = h * 2 * LANES
        width = min(2 * LANES, coef - first)
        total = out_ref[...]
        for k in range(offsets):
            total = total + nt_dot(m2l[k, :, first : first + width], cols[h, k, :, :width])
        out_ref[...] = total

    for c in range(chunks):
        for d in range(1, groups):
            relay(c, d).wait_send()
        for side, has in enumerate((has_after, has_before)):

            @pl.when(has)
            def _():
                hand(c, side).wait_send()


def body(multipole, dest, parent_local, parent_of, send_list, lists, m2l_ops, l2l_ops):
    groups, columns = lax.axis_size("grp"), lax.axis_size("nbr")
    coef, boxes = multipole.shape
    offsets, slots = lists.shape
    octants = l2l_ops.shape[0]
    rim = send_list.shape[1]
    parents = parent_local.shape[1]
    chunks = -(-coef // LANES)
    dest_row = dest.reshape(1, boxes)
    parent_rows = parent_local.T
    child_row = parent_of.reshape(1, slots)
    args = [
        pltpu.with_memory_space_constraint(a, pltpu.HBM)
        for a in (multipole, dest_row, parent_rows, child_row, send_list, lists, m2l_ops, l2l_ops)
    ]
    return pl.pallas_call(
        functools.partial(
            kernel, groups, columns, coef, boxes, slots, rim, parents, offsets, octants, chunks
        ),
        out_shape=jax.ShapeDtypeStruct((coef, slots), F32),
        in_specs=[pl.BlockSpec(memory_space=pltpu.HBM)] * len(args),
        out_specs=pl.BlockSpec(memory_space=pltpu.VMEM),
        scratch_shapes=[pltpu.VMEM(a.shape, a.dtype) for a in args]
        + [
            pltpu.VMEM((chunks, slots, LANES), BF16),
            pltpu.VMEM((chunks, slots, LANES), BF16),
            pltpu.VMEM((chunks, 2 * rim, LANES), BF16),
            pltpu.VMEM((chunks, 2 * rim, LANES), BF16),
            pltpu.VMEM((offsets, slots, slots + 2 * rim), BF16),
            pltpu.VMEM((chunks // 2, offsets, slots, 2 * LANES), BF16),
            pltpu.VMEM((octants, octants * parents, coef), BF16),
            pltpu.SemaphoreType.DMA((len(args),)),
            pltpu.SemaphoreType.DMA((chunks, groups - 1)),
            pltpu.SemaphoreType.DMA((chunks, groups - 1)),
            pltpu.SemaphoreType.DMA((chunks, 2)),
            pltpu.SemaphoreType.DMA((chunks, 2)),
            pltpu.SemaphoreType.REGULAR,
            pltpu.SemaphoreType.REGULAR,
        ],
        compiler_params=pltpu.CompilerParams(
            collective_id=0, has_side_effects=True, vmem_limit_bytes=48 * 1024 * 1024
        ),
        name="downward",
    )(*args)


def solution(mesh):
    placed = (
        P(None, ("grp", "nbr")),
        P(("grp", "nbr"), None),
        P(None, ("grp", "nbr")),
        P(("grp", "nbr")),
        P(None, ("grp", "nbr")),
        P(None, ("grp", "nbr")),
        P(),
        P(),
    )
    return jax.shard_map(
        body, mesh=mesh, in_specs=placed, out_specs=P(None, ("grp", "nbr")), check_vma=False
    )
```

```python
import functools

import jax
import jax.numpy as jnp
from jax import lax
from jax.experimental import pallas as pl
from jax.experimental.pallas import tpu as pltpu
from jax.sharding import PartitionSpec as P

MESH = pl.DeviceIdType.MESH
LANES = 128
WIDTH = 256
HALF = 256
F32 = jnp.float32
BF16 = jnp.bfloat16


def nt_dot(a, b):
    return lax.dot_general(a, b, (((1,), (1,)), ((), ())), preferred_element_type=F32)


def nn_dot(a, b):
    return jnp.dot(a, b, preferred_element_type=F32)


def iota(shape, dim):
    return lax.broadcasted_iota(jnp.int32, shape, dim)


def as_bf16(mask):
    return jnp.where(mask, jnp.ones((), F32), jnp.zeros((), F32)).astype(BF16)


def down_columns(row):
    return jnp.transpose(jnp.broadcast_to(row, (LANES, row.shape[1])))


def kernel(
    groups, columns, coef, boxes, slots, rim, parents, offsets, octants, chunks,
    mult_hbm, dest_hbm, par_hbm, pof_hbm, send_hbm, list_hbm, m2l_hbm, l2l_hbm,
    out_ref,
    mult, dest, par, pof, send, entries, m2l, l2l,
    outgoing, own, offer, near, hot, cols, blocks,
    in_sem, a_send, a_recv, n_send, n_recv, group_in, first_in, columns_in,
):
    cap = slots // groups
    per = HALF // WIDTH
    halves = chunks // per
    g = lax.axis_index("grp")
    n = lax.axis_index("nbr")
    after, before = n + 1, n - 1
    has_after, has_before = n < columns - 1, n > 0

    loads = [
        pltpu.make_async_copy(src, dst, in_sem.at[i])
        for i, (src, dst) in enumerate(
            (
                (dest_hbm, dest),
                (mult_hbm, mult),
                (send_hbm, send),
                (list_hbm, entries),
                (par_hbm, par),
                (pof_hbm, pof),
                (l2l_hbm, l2l),
                (m2l_hbm, m2l),
            )
        )
    ]
    for load in loads:
        load.start()

    barrier = pltpu.get_barrier_semaphore()

    def tell(semaphore, member, column):
        pl.semaphore_signal(semaphore, inc=1, device_id=(member, column), device_id_type=MESH)

    @pl.when(g == 0)
    def _():
        tell(barrier, 1, n)

    @pl.when((g == 1) | (g > 2))
    def _():
        tell(barrier, 2, n)

    for has, to in ((has_after, after), (has_before, before)):

        @pl.when(has)
        def _():
            tell(barrier, jnp.where((g == 1) | (g == 2), g + 2, g), to)

    loads[0].wait()
    owner = dest[...]
    named = iota((groups, boxes), 0) == owner
    earlier = as_bf16(iota((boxes, boxes), 0) < iota((boxes, boxes), 1))
    counts = nn_dot(as_bf16(named), earlier)
    arrival = jnp.sum(jnp.where(named, counts, jnp.zeros_like(counts)), axis=0, keepdims=True)
    position = owner * cap + arrival.astype(jnp.int32)
    placing = as_bf16(iota((slots, boxes), 0) == position)

    outgoing[chunks - 1] = jnp.zeros((slots, WIDTH), BF16)
    loads[1].wait()
    placed = nt_dot(placing, mult[...]).astype(BF16)
    for c in range(chunks):
        width = min(WIDTH, coef - c * WIDTH)
        outgoing[c, :, :width] = placed[:, c * WIDTH : c * WIDTH + width]
    mine = pl.ds(pl.multiple_of(g * cap, cap), cap)
    for c in range(chunks):
        own[c, mine, :] = outgoing[c, mine, :]

    def relay(c, d):
        to = lax.rem(g + d, groups)
        return pltpu.make_async_remote_copy(
            src_ref=outgoing.at[c, pl.ds(pl.multiple_of(to * cap, cap), cap)],
            dst_ref=own.at[c, mine],
            send_sem=a_send.at[c, d - 1],
            recv_sem=a_recv.at[c, d - 1],
            device_id=(to, n),
            device_id_type=MESH,
        )

    def hand(c, side):
        return pltpu.make_async_remote_copy(
            src_ref=offer.at[c, pl.ds(side * rim, rim)],
            dst_ref=near.at[c, pl.ds(side * rim, rim)],
            send_sem=n_send.at[c, side],
            recv_sem=n_recv.at[c, side],
            device_id=(g, (after, before)[side]),
            device_id_type=MESH,
        )

    loads[2].wait()
    lane = iota((rim, LANES), 1)
    picks = []
    for side in range(2):
        wanted = down_columns(send[side : side + 1, :])
        picks.append(
            jnp.concatenate(
                [as_bf16(wanted == lane + t * LANES) for t in range(slots // LANES)], axis=1
            )
        )
    pick = jnp.concatenate(picks, axis=0)

    loads[3].wait()
    listed = entries[...]
    from_left = (listed >= slots) & (listed < slots + rim)
    from_right = listed >= slots + rim
    listed = jnp.where(from_left & (n == 0), -1, listed)
    entries[...] = jnp.where(from_right & (n == columns - 1), -1, listed)
    slot_lane = iota((slots, LANES), 1)

    def build(k):
        wanted = down_columns(entries[k : k + 1, :])
        for t in range(hot.shape[2] // LANES):
            hot[k, :, t * LANES : (t + 1) * LANES] = as_bf16(wanted == slot_lane + t * LANES)

    def know_columns():
        ends = columns - 1
        beside = (n + ends) // columns + (ends - n + ends) // columns

        @pl.when((g == 0) | (g > 4))
        def _():
            pl.semaphore_wait(barrier, beside)

        @pl.when((g == 3) | (g == 4))
        def _():
            pl.semaphore_wait(barrier, 2 * beside)
            tell(columns_in, g - 2, n)

        @pl.when((g == 1) | (g == 2))
        def _():
            pl.semaphore_wait(columns_in, 1)

    def pass_on(c):
        for d in range(1, groups):
            relay(c, d).wait_recv()
        offer[c] = nn_dot(pick, own[c]).astype(BF16)
        if c == 0:
            know_columns()
        for side, has in enumerate((has_after, has_before)):

            @pl.when(has)
            def _():
                hand(c, side).start()

    def half_of(ref, h):
        return jnp.concatenate([ref[per * h + i] for i in range(per)], axis=1)

    def from_own(h):
        local = half_of(own, h)
        for k in range(offsets):
            cols[h, k] = nn_dot(hot[k, :, :slots], local).astype(BF16)

    for k in range(offsets):
        build(k)

    @pl.when(g == 2)
    def _():
        pl.semaphore_wait(barrier, groups - 2)
        for member in range(1, groups):
            if member != 2:
                tell(group_in, member, n)

    @pl.when((g == 1) | (g > 2))
    def _():
        pl.semaphore_wait(group_in, 1)

    for c in range(chunks):
        for d in range(1, groups):

            @pl.when((g > 0) & (g + d != groups))
            def _():
                relay(c, d).start()

    @pl.when(g == 1)
    def _():
        pl.semaphore_wait(barrier, 1)
        for member in range(groups):
            if member != 1:
                tell(first_in, member, n)

    @pl.when(g != 1)
    def _():
        pl.semaphore_wait(first_in, 1)

    for c in range(chunks):
        for d in range(1, groups):

            @pl.when((g == 0) | (g + d == groups))
            def _():
                relay(c, d).start()

    for i in (4, 5, 6):
        loads[i].wait()
    blocks[...] = jnp.zeros(blocks.shape, BF16)
    for q in range(octants):
        blocks[q, pl.ds(q * parents, parents), :] = par[...]
    translated = nt_dot(l2l[0], blocks[0])
    for q in range(1, octants):
        translated = translated + nt_dot(l2l[q], blocks[q])
    upper = translated.astype(BF16)
    lower = (translated - upper.astype(F32)).astype(BF16)
    child = as_bf16(iota((octants * parents, slots), 0) == pof[...])
    out_ref[...] = nn_dot(upper, child) + nn_dot(lower, child)
    for h in range(halves):
        for c in range(per * h, per * h + per):
            pass_on(c)
        from_own(h)

    @pl.when(n == 0)
    def _():
        near[:, :rim] = jnp.zeros((chunks, rim, WIDTH), BF16)

    @pl.when(n == columns - 1)
    def _():
        near[:, rim:] = jnp.zeros((chunks, rim, WIDTH), BF16)

    loads[7].wait()
    for h in range(halves):
        for c in range(per * h, per * h + per):
            for side, has in enumerate((has_before, has_after)):

                @pl.when(has)
                def _():
                    hand(c, side).wait_recv()

        beside = half_of(near, h)
        for k in range(offsets):
            cols[h, k] = cols[h, k] + nn_dot(hot[k, :, slots:], beside).astype(BF16)
        first = h * HALF
        width = min(HALF, coef - first)
        total = out_ref[...]
        for k in range(offsets):
            total = total + nt_dot(m2l[k, :, first : first + width], cols[h, k, :, :width])
        out_ref[...] = total

    for c in range(chunks):
        for d in range(1, groups):
            relay(c, d).wait_send()
        for side, has in enumerate((has_after, has_before)):

            @pl.when(has)
            def _():
                hand(c, side).wait_send()


def body(multipole, dest, parent_local, parent_of, send_list, lists, m2l_ops, l2l_ops):
    groups, columns = lax.axis_size("grp"), lax.axis_size("nbr")
    coef, boxes = multipole.shape
    offsets, slots = lists.shape
    octants = l2l_ops.shape[0]
    rim = send_list.shape[1]
    parents = parent_local.shape[1]
    chunks = -(-coef // HALF) * (HALF // WIDTH)
    dest_row = dest.reshape(1, boxes)
    parent_rows = parent_local.T
    child_row = parent_of.reshape(1, slots)
    args = [
        pltpu.with_memory_space_constraint(a, pltpu.HBM)
        for a in (multipole, dest_row, parent_rows, child_row, send_list, lists, m2l_ops, l2l_ops)
    ]
    return pl.pallas_call(
        functools.partial(
            kernel, groups, columns, coef, boxes, slots, rim, parents, offsets, octants, chunks
        ),
        out_shape=jax.ShapeDtypeStruct((coef, slots), F32),
        in_specs=[pl.BlockSpec(memory_space=pltpu.HBM)] * len(args),
        out_specs=pl.BlockSpec(memory_space=pltpu.VMEM),
        scratch_shapes=[pltpu.VMEM(a.shape, a.dtype) for a in args]
        + [
            pltpu.VMEM((chunks, slots, WIDTH), BF16),
            pltpu.VMEM((chunks, slots, WIDTH), BF16),
            pltpu.VMEM((chunks, 2 * rim, WIDTH), BF16),
            pltpu.VMEM((chunks, 2 * rim, WIDTH), BF16),
            pltpu.VMEM((offsets, slots, slots + 2 * rim), BF16),
            pltpu.VMEM((-(-coef // HALF), offsets, slots, HALF), BF16),
            pltpu.VMEM((octants, octants * parents, coef), BF16),
            pltpu.SemaphoreType.DMA((len(args),)),
            pltpu.SemaphoreType.DMA((chunks, groups - 1)),
            pltpu.SemaphoreType.DMA((chunks, groups - 1)),
            pltpu.SemaphoreType.DMA((chunks, 2)),
            pltpu.SemaphoreType.DMA((chunks, 2)),
            pltpu.SemaphoreType.REGULAR,
            pltpu.SemaphoreType.REGULAR,
            pltpu.SemaphoreType.REGULAR,
        ],
        compiler_params=pltpu.CompilerParams(
            collective_id=0, has_side_effects=True, vmem_limit_bytes=48 * 1024 * 1024
        ),
        name="downward",
    )(*args)


def solution(mesh):
    placed = (
        P(None, ("grp", "nbr")),
        P(("grp", "nbr"), None),
        P(None, ("grp", "nbr")),
        P(("grp", "nbr")),
        P(None, ("grp", "nbr")),
        P(None, ("grp", "nbr")),
        P(),
        P(),
    )
    return jax.shard_map(
        body, mesh=mesh, in_specs=placed, out_specs=P(None, ("grp", "nbr")), check_vma=False
    )
```

```python
import functools

import jax
import jax.numpy as jnp
from jax import lax
from jax.experimental import pallas as pl
from jax.experimental.pallas import tpu as pltpu
from jax.sharding import PartitionSpec as P

MESH = pl.DeviceIdType.MESH
LANES = 128
WIDTH = 256
HALF = 256
F32 = jnp.float32
BF16 = jnp.bfloat16


def nt_dot(a, b):
    return lax.dot_general(a, b, (((1,), (1,)), ((), ())), preferred_element_type=F32)


def nn_dot(a, b):
    return jnp.dot(a, b, preferred_element_type=F32)


def iota(shape, dim):
    return lax.broadcasted_iota(jnp.int32, shape, dim)


def as_bf16(mask):
    return jnp.where(mask, jnp.ones((), F32), jnp.zeros((), F32)).astype(BF16)


def down_columns(row):
    return jnp.transpose(jnp.broadcast_to(row, (LANES, row.shape[1])))


def kernel(
    groups, columns, coef, boxes, slots, rim, parents, offsets, octants, chunks,
    mult_hbm, dest_hbm, par_hbm, pof_hbm, send_hbm, list_hbm, m2l_hbm, l2l_hbm,
    out_ref,
    mult, dest, par, pof, send, entries, m2l, l2l,
    outgoing, own, offer, near, hot, cols, blocks,
    in_sem, a_send, a_recv, n_send, n_recv, group_in, first_in, columns_in,
):
    cap = slots // groups
    per = HALF // WIDTH
    halves = chunks // per
    g = lax.axis_index("grp")
    n = lax.axis_index("nbr")
    after, before = n + 1, n - 1
    has_after, has_before = n < columns - 1, n > 0
    apart = n == 0

    loads = [
        pltpu.make_async_copy(src, dst, in_sem.at[i])
        for i, (src, dst) in enumerate(
            (
                (dest_hbm, dest),
                (mult_hbm, mult),
                (send_hbm, send),
                (list_hbm, entries),
                (par_hbm, par),
                (pof_hbm, pof),
                (l2l_hbm, l2l),
                (m2l_hbm, m2l),
            )
        )
    ]
    for load in loads:
        load.start()

    barrier = pltpu.get_barrier_semaphore()

    def tell(semaphore, member, column):
        pl.semaphore_signal(semaphore, inc=1, device_id=(member, column), device_id_type=MESH)

    @pl.when(g == 0)
    def _():
        tell(barrier, jnp.where(apart, 1, 2), n)

    @pl.when((g == 1) | (g > 2))
    def _():
        tell(barrier, 2, n)

    for has, to in ((has_after, after), (has_before, before)):

        @pl.when(has)
        def _():
            tell(barrier, jnp.where((g == 1) | (g == 2), g + 2, g), to)

    loads[0].wait()
    owner = dest[...]
    named = iota((groups, boxes), 0) == owner
    earlier = as_bf16(iota((boxes, boxes), 0) < iota((boxes, boxes), 1))
    counts = nn_dot(as_bf16(named), earlier)
    arrival = jnp.sum(jnp.where(named, counts, jnp.zeros_like(counts)), axis=0, keepdims=True)
    position = owner * cap + arrival.astype(jnp.int32)
    placing = as_bf16(iota((slots, boxes), 0) == position)

    outgoing[chunks - 1] = jnp.zeros((slots, WIDTH), BF16)
    loads[1].wait()
    placed = nt_dot(placing, mult[...]).astype(BF16)
    for c in range(chunks):
        width = min(WIDTH, coef - c * WIDTH)
        outgoing[c, :, :width] = placed[:, c * WIDTH : c * WIDTH + width]
    mine = pl.ds(pl.multiple_of(g * cap, cap), cap)
    for c in range(chunks):
        own[c, mine, :] = outgoing[c, mine, :]

    def relay(c, d):
        to = lax.rem(g + d, groups)
        return pltpu.make_async_remote_copy(
            src_ref=outgoing.at[c, pl.ds(pl.multiple_of(to * cap, cap), cap)],
            dst_ref=own.at[c, mine],
            send_sem=a_send.at[c, d - 1],
            recv_sem=a_recv.at[c, d - 1],
            device_id=(to, n),
            device_id_type=MESH,
        )

    def hand(c, side):
        return pltpu.make_async_remote_copy(
            src_ref=offer.at[c, pl.ds(side * rim, rim)],
            dst_ref=near.at[c, pl.ds(side * rim, rim)],
            send_sem=n_send.at[c, side],
            recv_sem=n_recv.at[c, side],
            device_id=(g, (after, before)[side]),
            device_id_type=MESH,
        )

    loads[2].wait()
    lane = iota((rim, LANES), 1)
    picks = []
    for side in range(2):
        wanted = down_columns(send[side : side + 1, :])
        picks.append(
            jnp.concatenate(
                [as_bf16(wanted == lane + t * LANES) for t in range(slots // LANES)], axis=1
            )
        )
    pick = jnp.concatenate(picks, axis=0)

    loads[3].wait()
    listed = entries[...]
    from_left = (listed >= slots) & (listed < slots + rim)
    from_right = listed >= slots + rim
    listed = jnp.where(from_left & (n == 0), -1, listed)
    entries[...] = jnp.where(from_right & (n == columns - 1), -1, listed)
    slot_lane = iota((slots, LANES), 1)

    def build(k):
        wanted = down_columns(entries[k : k + 1, :])
        for t in range(hot.shape[2] // LANES):
            hot[k, :, t * LANES : (t + 1) * LANES] = as_bf16(wanted == slot_lane + t * LANES)

    def know_columns():
        ends = columns - 1
        beside = (n + ends) // columns + (ends - n + ends) // columns

        @pl.when((g == 0) | (g > 4))
        def _():
            pl.semaphore_wait(barrier, beside)

        @pl.when((g == 3) | (g == 4))
        def _():
            pl.semaphore_wait(barrier, 2 * beside)
            tell(columns_in, g - 2, n)

        @pl.when((g == 1) | (g == 2))
        def _():
            pl.semaphore_wait(columns_in, 1)

    def pass_on(c):
        for d in range(1, groups):
            relay(c, d).wait_recv()
        offer[c] = nn_dot(pick, own[c]).astype(BF16)
        if c == 0:
            know_columns()
        for side, has in enumerate((has_after, has_before)):

            @pl.when(has)
            def _():
                hand(c, side).start()

    def half_of(ref, h):
        return jnp.concatenate([ref[per * h + i] for i in range(per)], axis=1)

    def from_own(h):
        local = half_of(own, h)
        for k in range(offsets):
            cols[h, k] = nn_dot(hot[k, :, :slots], local).astype(BF16)

    @pl.when((g == 2) & apart)
    def _():
        pl.semaphore_wait(barrier, groups - 2)
        for member in range(1, groups):
            if member != 2:
                tell(group_in, member, n)

    @pl.when((g == 2) & (n > 0))
    def _():
        pl.semaphore_wait(barrier, groups - 1)
        for member in range(groups):
            if member != 2:
                tell(group_in, member, n)

    @pl.when((g == 1) | (g > 2) | ((g == 0) & (n > 0)))
    def _():
        pl.semaphore_wait(group_in, 1)

    for c in range(chunks):
        for d in range(1, groups):

            @pl.when((n > 0) | ((g > 0) & (g + d != groups)))
            def _():
                relay(c, d).start()

    @pl.when((g == 0) & apart)
    def _():
        pl.semaphore_wait(first_in, 1)
        for c in range(chunks):
            for d in range(1, groups):
                relay(c, d).start()

    for k in range(offsets):
        build(k)

    for i in (4, 5, 6):
        loads[i].wait()
    blocks[...] = jnp.zeros(blocks.shape, BF16)
    for q in range(octants):
        blocks[q, pl.ds(q * parents, parents), :] = par[...]
    translated = nt_dot(l2l[0], blocks[0])
    for q in range(1, octants):
        translated = translated + nt_dot(l2l[q], blocks[q])
    upper = translated.astype(BF16)
    lower = (translated - upper.astype(F32)).astype(BF16)
    child = as_bf16(iota((octants * parents, slots), 0) == pof[...])
    out_ref[...] = nn_dot(upper, child) + nn_dot(lower, child)
    @pl.when((g == 1) & apart)
    def _():
        pl.semaphore_wait(barrier, 1)
        for member in range(groups):
            if member != 1:
                tell(first_in, member, n)

    @pl.when((g > 1) & apart)
    def _():
        pl.semaphore_wait(first_in, 1)

    @pl.when((g > 0) & apart)
    def _():
        for c in range(chunks):
            relay(c, groups - g).start()

    for h in range(halves):
        for c in range(per * h, per * h + per):
            pass_on(c)
        from_own(h)

    @pl.when(n == 0)
    def _():
        near[:, :rim] = jnp.zeros((chunks, rim, WIDTH), BF16)

    @pl.when(n == columns - 1)
    def _():
        near[:, rim:] = jnp.zeros((chunks, rim, WIDTH), BF16)

    loads[7].wait()
    for h in range(halves):
        for c in range(per * h, per * h + per):
            for side, has in enumerate((has_before, has_after)):

                @pl.when(has)
                def _():
                    hand(c, side).wait_recv()

        beside = half_of(near, h)
        for k in range(offsets):
            cols[h, k] = cols[h, k] + nn_dot(hot[k, :, slots:], beside).astype(BF16)
        first = h * HALF
        width = min(HALF, coef - first)
        total = out_ref[...]
        for k in range(offsets):
            total = total + nt_dot(m2l[k, :, first : first + width], cols[h, k, :, :width])
        out_ref[...] = total

    for c in range(chunks):
        for d in range(1, groups):
            relay(c, d).wait_send()
        for side, has in enumerate((has_after, has_before)):

            @pl.when(has)
            def _():
                hand(c, side).wait_send()


def body(multipole, dest, parent_local, parent_of, send_list, lists, m2l_ops, l2l_ops):
    groups, columns = lax.axis_size("grp"), lax.axis_size("nbr")
    coef, boxes = multipole.shape
    offsets, slots = lists.shape
    octants = l2l_ops.shape[0]
    rim = send_list.shape[1]
    parents = parent_local.shape[1]
    chunks = -(-coef // HALF) * (HALF // WIDTH)
    dest_row = dest.reshape(1, boxes)
    parent_rows = parent_local.T
    child_row = parent_of.reshape(1, slots)
    args = [
        pltpu.with_memory_space_constraint(a, pltpu.HBM)
        for a in (multipole, dest_row, parent_rows, child_row, send_list, lists, m2l_ops, l2l_ops)
    ]
    return pl.pallas_call(
        functools.partial(
            kernel, groups, columns, coef, boxes, slots, rim, parents, offsets, octants, chunks
        ),
        out_shape=jax.ShapeDtypeStruct((coef, slots), F32),
        in_specs=[pl.BlockSpec(memory_space=pltpu.HBM)] * len(args),
        out_specs=pl.BlockSpec(memory_space=pltpu.VMEM),
        scratch_shapes=[pltpu.VMEM(a.shape, a.dtype) for a in args]
        + [
            pltpu.VMEM((chunks, slots, WIDTH), BF16),
            pltpu.VMEM((chunks, slots, WIDTH), BF16),
            pltpu.VMEM((chunks, 2 * rim, WIDTH), BF16),
            pltpu.VMEM((chunks, 2 * rim, WIDTH), BF16),
            pltpu.VMEM((offsets, slots, slots + 2 * rim), BF16),
            pltpu.VMEM((-(-coef // HALF), offsets, slots, HALF), BF16),
            pltpu.VMEM((octants, octants * parents, coef), BF16),
            pltpu.SemaphoreType.DMA((len(args),)),
            pltpu.SemaphoreType.DMA((chunks, groups - 1)),
            pltpu.SemaphoreType.DMA((chunks, groups - 1)),
            pltpu.SemaphoreType.DMA((chunks, 2)),
            pltpu.SemaphoreType.DMA((chunks, 2)),
            pltpu.SemaphoreType.REGULAR,
            pltpu.SemaphoreType.REGULAR,
            pltpu.SemaphoreType.REGULAR,
        ],
        compiler_params=pltpu.CompilerParams(
            collective_id=0, has_side_effects=True, vmem_limit_bytes=48 * 1024 * 1024
        ),
        name="downward",
    )(*args)


def solution(mesh):
    placed = (
        P(None, ("grp", "nbr")),
        P(("grp", "nbr"), None),
        P(None, ("grp", "nbr")),
        P(("grp", "nbr")),
        P(None, ("grp", "nbr")),
        P(None, ("grp", "nbr")),
        P(),
        P(),
    )
    return jax.shard_map(
        body, mesh=mesh, in_specs=placed, out_specs=P(None, ("grp", "nbr")), check_vma=False
    )
```

```python
import functools

import jax
import jax.numpy as jnp
from jax import lax
from jax.experimental import pallas as pl
from jax.experimental.pallas import tpu as pltpu
from jax.sharding import PartitionSpec as P

MESH = pl.DeviceIdType.MESH
LANES = 128
WIDTH = 256
HALF = 256
F32 = jnp.float32
BF16 = jnp.bfloat16


def nt_dot(a, b):
    return lax.dot_general(a, b, (((1,), (1,)), ((), ())), preferred_element_type=F32)


def nn_dot(a, b):
    return jnp.dot(a, b, preferred_element_type=F32)


def iota(shape, dim):
    return lax.broadcasted_iota(jnp.int32, shape, dim)


def as_bf16(mask):
    return jnp.where(mask, jnp.ones((), F32), jnp.zeros((), F32)).astype(BF16)


def down_columns(row):
    return jnp.transpose(jnp.broadcast_to(row, (LANES, row.shape[1])))


def kernel(
    groups, columns, coef, boxes, slots, rim, parents, offsets, octants, chunks,
    mult_hbm, dest_hbm, par_hbm, pof_hbm, send_hbm, list_hbm, m2l_hbm, l2l_hbm,
    out_ref,
    mult, dest, par, pof, send, entries, m2l, l2l,
    outgoing, own, offer, near, hot, cols, blocks,
    in_sem, a_send, a_recv, n_send, n_recv, group_in, first_in, before_in, after_in,
):
    cap = slots // groups
    per = HALF // WIDTH
    halves = chunks // per
    g = lax.axis_index("grp")
    n = lax.axis_index("nbr")
    after, before = lax.rem(n + 1, columns), lax.rem(n + columns - 1, columns)
    has_after, has_before = n < columns - 1, n > 0
    apart = n == 0

    loads = [
        pltpu.make_async_copy(src, dst, in_sem.at[i])
        for i, (src, dst) in enumerate(
            (
                (dest_hbm, dest),
                (mult_hbm, mult),
                (send_hbm, send),
                (list_hbm, entries),
                (par_hbm, par),
                (pof_hbm, pof),
                (l2l_hbm, l2l),
                (m2l_hbm, m2l),
            )
        )
    ]
    for load in loads:
        load.start()

    barrier = pltpu.get_barrier_semaphore()

    def tell(semaphore, member, column):
        pl.semaphore_signal(semaphore, inc=1, device_id=(member, column), device_id_type=MESH)

    for d in range(1, groups):
        member = lax.rem(g + d, groups)

        @pl.when((n > 0) & (member != 0) & (member != 4))
        def _():
            tell(barrier, member, n)

    @pl.when((g == 0) & apart)
    def _():
        tell(barrier, 1, n)

    @pl.when(((g == 1) | (g > 2)) & apart)
    def _():
        tell(barrier, 2, n)

    for has, to, member in ((has_after, after, 0), (has_before, before, 4)):

        @pl.when(has)
        def _():
            tell(barrier, member, to)

    loads[0].wait()
    owner = dest[...]
    named = iota((groups, boxes), 0) == owner
    earlier = as_bf16(iota((boxes, boxes), 0) < iota((boxes, boxes), 1))
    counts = nn_dot(as_bf16(named), earlier)
    arrival = jnp.sum(jnp.where(named, counts, jnp.zeros_like(counts)), axis=0, keepdims=True)
    position = owner * cap + arrival.astype(jnp.int32)
    placing = as_bf16(iota((slots, boxes), 0) == position)

    outgoing[chunks - 1] = jnp.zeros((slots, WIDTH), BF16)
    loads[1].wait()
    placed = nt_dot(placing, mult[...]).astype(BF16)
    for c in range(chunks):
        width = min(WIDTH, coef - c * WIDTH)
        outgoing[c, :, :width] = placed[:, c * WIDTH : c * WIDTH + width]
    mine = pl.ds(pl.multiple_of(g * cap, cap), cap)
    for c in range(chunks):
        own[c, mine, :] = outgoing[c, mine, :]

    def relay(c, d):
        to = lax.rem(g + d, groups)
        return pltpu.make_async_remote_copy(
            src_ref=outgoing.at[c, pl.ds(pl.multiple_of(to * cap, cap), cap)],
            dst_ref=own.at[c, mine],
            send_sem=a_send.at[c, d - 1],
            recv_sem=a_recv.at[c, d - 1],
            device_id=(to, n),
            device_id_type=MESH,
        )

    def hand(c, side):
        return pltpu.make_async_remote_copy(
            src_ref=offer.at[c, pl.ds(side * rim, rim)],
            dst_ref=near.at[c, pl.ds(side * rim, rim)],
            send_sem=n_send.at[c, side],
            recv_sem=n_recv.at[c, side],
            device_id=(g, (after, before)[side]),
            device_id_type=MESH,
        )

    loads[2].wait()
    lane = iota((rim, LANES), 1)
    picks = []
    for side in range(2):
        wanted = down_columns(send[side : side + 1, :])
        picks.append(
            jnp.concatenate(
                [as_bf16(wanted == lane + t * LANES) for t in range(slots // LANES)], axis=1
            )
        )
    pick = jnp.concatenate(picks, axis=0)

    loads[3].wait()
    listed = entries[...]
    from_left = (listed >= slots) & (listed < slots + rim)
    from_right = listed >= slots + rim
    listed = jnp.where(from_left & (n == 0), -1, listed)
    entries[...] = jnp.where(from_right & (n == columns - 1), -1, listed)
    slot_lane = iota((slots, LANES), 1)

    def build(k):
        wanted = down_columns(entries[k : k + 1, :])
        for t in range(hot.shape[2] // LANES):
            hot[k, :, t * LANES : (t + 1) * LANES] = as_bf16(wanted == slot_lane + t * LANES)

    sides = ((1, has_before, 0, before_in), (0, has_after, 4, after_in))

    def hear_columns():
        for _, has, listener, semaphore in sides:

            @pl.when((g == listener) & has)
            def _():
                pl.semaphore_wait(barrier, groups)
                for member in range(groups):
                    if member != listener:
                        tell(semaphore, member, n)

    def know_column(has, listener, semaphore):
        @pl.when((g != listener) & has)
        def _():
            pl.semaphore_wait(semaphore, 1)

    def pass_on(c):
        for d in range(1, groups):
            relay(c, d).wait_recv()
        offer[c] = nn_dot(pick, own[c]).astype(BF16)
        for side, has, listener, semaphore in sides:
            if c == 0:
                know_column(has, listener, semaphore)

            @pl.when(has)
            def _():
                hand(c, side).start()

    def half_of(ref, h):
        return jnp.concatenate([ref[per * h + i] for i in range(per)], axis=1)

    def from_own(h):
        local = half_of(own, h)
        for k in range(offsets):
            cols[h, k] = nn_dot(hot[k, :, :slots], local).astype(BF16)

    @pl.when((g == 2) & apart)
    def _():
        pl.semaphore_wait(barrier, groups - 2)
        for member in range(1, groups):
            if member != 2:
                tell(group_in, member, n)

    @pl.when((g != 0) & (g != 4) & (n > 0))
    def _():
        pl.semaphore_wait(barrier, groups - 1)

    @pl.when(((g == 1) | (g == 5)) & (n > 0))
    def _():
        tell(group_in, g - 1, n)

    @pl.when(((g == 0) | (g == 4)) & (n > 0))
    def _():
        pl.semaphore_wait(group_in, 1)

    @pl.when(((g == 1) | (g > 2)) & apart)
    def _():
        pl.semaphore_wait(group_in, 1)

    for c in range(chunks):
        for d in range(1, groups):

            @pl.when((n > 0) | ((g > 0) & (g + d != groups)))
            def _():
                relay(c, d).start()

    @pl.when((g == 0) & apart)
    def _():
        pl.semaphore_wait(first_in, 1)
        for c in range(chunks):
            for d in range(1, groups):
                relay(c, d).start()

    for k in range(offsets):
        build(k)

    for i in (4, 5, 6):
        loads[i].wait()
    blocks[...] = jnp.zeros(blocks.shape, BF16)
    for q in range(octants):
        blocks[q, pl.ds(q * parents, parents), :] = par[...]
    translated = nt_dot(l2l[0], blocks[0])
    for q in range(1, octants):
        translated = translated + nt_dot(l2l[q], blocks[q])
    upper = translated.astype(BF16)
    lower = (translated - upper.astype(F32)).astype(BF16)
    child = as_bf16(iota((octants * parents, slots), 0) == pof[...])
    out_ref[...] = nn_dot(upper, child) + nn_dot(lower, child)
    @pl.when((g == 1) & apart)
    def _():
        pl.semaphore_wait(barrier, 1)
        for member in range(groups):
            if member != 1:
                tell(first_in, member, n)

    @pl.when((g > 1) & apart)
    def _():
        pl.semaphore_wait(first_in, 1)

    @pl.when((g > 0) & apart)
    def _():
        for c in range(chunks):
            relay(c, groups - g).start()

    hear_columns()
    for h in range(halves):
        for c in range(per * h, per * h + per):
            pass_on(c)
        from_own(h)

    @pl.when(n == 0)
    def _():
        near[:, :rim] = jnp.zeros((chunks, rim, WIDTH), BF16)

    @pl.when(n == columns - 1)
    def _():
        near[:, rim:] = jnp.zeros((chunks, rim, WIDTH), BF16)

    loads[7].wait()
    for h in range(halves):
        for c in range(per * h, per * h + per):
            for side, has in enumerate((has_before, has_after)):

                @pl.when(has)
                def _():
                    hand(c, side).wait_recv()

        beside = half_of(near, h)
        for k in range(offsets):
            cols[h, k] = cols[h, k] + nn_dot(hot[k, :, slots:], beside).astype(BF16)
        first = h * HALF
        width = min(HALF, coef - first)
        total = out_ref[...]
        for k in range(offsets):
            total = total + nt_dot(m2l[k, :, first : first + width], cols[h, k, :, :width])
        out_ref[...] = total

    for c in range(chunks):
        for d in range(1, groups):
            relay(c, d).wait_send()
        for side, has in enumerate((has_after, has_before)):

            @pl.when(has)
            def _():
                hand(c, side).wait_send()


def body(multipole, dest, parent_local, parent_of, send_list, lists, m2l_ops, l2l_ops):
    groups, columns = lax.axis_size("grp"), lax.axis_size("nbr")
    coef, boxes = multipole.shape
    offsets, slots = lists.shape
    octants = l2l_ops.shape[0]
    rim = send_list.shape[1]
    parents = parent_local.shape[1]
    chunks = -(-coef // HALF) * (HALF // WIDTH)
    dest_row = dest.reshape(1, boxes)
    parent_rows = parent_local.T
    child_row = parent_of.reshape(1, slots)
    args = [
        pltpu.with_memory_space_constraint(a, pltpu.HBM)
        for a in (multipole, dest_row, parent_rows, child_row, send_list, lists, m2l_ops, l2l_ops)
    ]
    return pl.pallas_call(
        functools.partial(
            kernel, groups, columns, coef, boxes, slots, rim, parents, offsets, octants, chunks
        ),
        out_shape=jax.ShapeDtypeStruct((coef, slots), F32),
        in_specs=[pl.BlockSpec(memory_space=pltpu.HBM)] * len(args),
        out_specs=pl.BlockSpec(memory_space=pltpu.VMEM),
        scratch_shapes=[pltpu.VMEM(a.shape, a.dtype) for a in args]
        + [
            pltpu.VMEM((chunks, slots, WIDTH), BF16),
            pltpu.VMEM((chunks, slots, WIDTH), BF16),
            pltpu.VMEM((chunks, 2 * rim, WIDTH), BF16),
            pltpu.VMEM((chunks, 2 * rim, WIDTH), BF16),
            pltpu.VMEM((offsets, slots, slots + 2 * rim), BF16),
            pltpu.VMEM((-(-coef // HALF), offsets, slots, HALF), BF16),
            pltpu.VMEM((octants, octants * parents, coef), BF16),
            pltpu.SemaphoreType.DMA((len(args),)),
            pltpu.SemaphoreType.DMA((chunks, groups - 1)),
            pltpu.SemaphoreType.DMA((chunks, groups - 1)),
            pltpu.SemaphoreType.DMA((chunks, 2)),
            pltpu.SemaphoreType.DMA((chunks, 2)),
            pltpu.SemaphoreType.REGULAR,
            pltpu.SemaphoreType.REGULAR,
            pltpu.SemaphoreType.REGULAR,
            pltpu.SemaphoreType.REGULAR,
        ],
        compiler_params=pltpu.CompilerParams(
            collective_id=0, has_side_effects=True, vmem_limit_bytes=48 * 1024 * 1024
        ),
        name="downward",
    )(*args)


def solution(mesh):
    placed = (
        P(None, ("grp", "nbr")),
        P(("grp", "nbr"), None),
        P(None, ("grp", "nbr")),
        P(("grp", "nbr")),
        P(None, ("grp", "nbr")),
        P(None, ("grp", "nbr")),
        P(),
        P(),
    )
    return jax.shard_map(
        body, mesh=mesh, in_specs=placed, out_specs=P(None, ("grp", "nbr")), check_vma=False
    )
```

```python
import functools

import jax
import jax.numpy as jnp
from jax import lax
from jax.experimental import pallas as pl
from jax.experimental.pallas import tpu as pltpu
from jax.sharding import PartitionSpec as P

MESH = pl.DeviceIdType.MESH
LANES = 128
WIDTH = 256
HALF = 256
F32 = jnp.float32
BF16 = jnp.bfloat16


def nt_dot(a, b):
    return lax.dot_general(a, b, (((1,), (1,)), ((), ())), preferred_element_type=F32)


def nn_dot(a, b):
    return jnp.dot(a, b, preferred_element_type=F32)


def iota(shape, dim):
    return lax.broadcasted_iota(jnp.int32, shape, dim)


def as_bf16(mask):
    return jnp.where(mask, jnp.ones((), F32), jnp.zeros((), F32)).astype(BF16)


def down_columns(row):
    return jnp.transpose(jnp.broadcast_to(row, (LANES, row.shape[1])))


def kernel(
    groups, columns, coef, boxes, slots, rim, parents, offsets, octants, chunks,
    mult_hbm, dest_hbm, par_hbm, pof_hbm, send_hbm, list_hbm, m2l_hbm, l2l_hbm,
    out_ref,
    mult, dest, par, pof, send, entries, m2l, l2l,
    outgoing, own, offer, near, hot, cols, blocks,
    in_sem, a_send, a_recv, n_send, n_recv, group_in, first_in, before_in, after_in,
):
    cap = slots // groups
    per = HALF // WIDTH
    halves = chunks // per
    g = lax.axis_index("grp")
    n = lax.axis_index("nbr")
    after, before = lax.rem(n + 1, columns), lax.rem(n + columns - 1, columns)
    has_after, has_before = n < columns - 1, n > 0
    apart = n == 0

    loads = [
        pltpu.make_async_copy(src, dst, in_sem.at[i])
        for i, (src, dst) in enumerate(
            (
                (dest_hbm, dest),
                (mult_hbm, mult),
                (send_hbm, send),
                (list_hbm, entries),
                (par_hbm, par),
                (pof_hbm, pof),
                (l2l_hbm, l2l),
                (m2l_hbm, m2l),
            )
        )
    ]
    for load in loads:
        load.start()

    barrier = pltpu.get_barrier_semaphore()

    def tell(semaphore, member, column):
        pl.semaphore_signal(semaphore, inc=1, device_id=(member, column), device_id_type=MESH)

    for d in range(1, groups):
        member = lax.rem(g + d, groups)

        @pl.when((n > 0) & (member != 0) & (member != 4))
        def _():
            tell(barrier, member, n)

    @pl.when((g == 0) & apart)
    def _():
        tell(barrier, 1, n)

    @pl.when(((g == 1) | (g > 2)) & apart)
    def _():
        tell(barrier, 2, n)

    for has, to, member in ((has_after, after, 0), (has_before, before, 4)):

        @pl.when(has)
        def _():
            tell(barrier, member, to)

    loads[0].wait()
    owner = dest[...]
    named = iota((groups, boxes), 0) == owner
    earlier = as_bf16(iota((boxes, boxes), 0) < iota((boxes, boxes), 1))
    counts = nn_dot(as_bf16(named), earlier)
    arrival = jnp.sum(jnp.where(named, counts, jnp.zeros_like(counts)), axis=0, keepdims=True)
    position = owner * cap + arrival.astype(jnp.int32)
    placing = as_bf16(iota((slots, boxes), 0) == position)

    outgoing[chunks - 1] = jnp.zeros((slots, WIDTH), BF16)
    loads[1].wait()
    placed = nt_dot(placing, mult[...]).astype(BF16)
    for c in range(chunks):
        width = min(WIDTH, coef - c * WIDTH)
        outgoing[c, :, :width] = placed[:, c * WIDTH : c * WIDTH + width]
    mine = pl.ds(pl.multiple_of(g * cap, cap), cap)
    for c in range(chunks):
        own[c, mine, :] = outgoing[c, mine, :]

    def relay(c, d):
        to = lax.rem(g + d, groups)
        return pltpu.make_async_remote_copy(
            src_ref=outgoing.at[c, pl.ds(pl.multiple_of(to * cap, cap), cap)],
            dst_ref=own.at[c, mine],
            send_sem=a_send.at[c, d - 1],
            recv_sem=a_recv.at[c, d - 1],
            device_id=(to, n),
            device_id_type=MESH,
        )

    def hand(c, side):
        return pltpu.make_async_remote_copy(
            src_ref=offer.at[c, pl.ds(side * rim, rim)],
            dst_ref=near.at[c, pl.ds(side * rim, rim)],
            send_sem=n_send.at[c, side],
            recv_sem=n_recv.at[c, side],
            device_id=(g, (after, before)[side]),
            device_id_type=MESH,
        )

    loads[2].wait()
    lane = iota((rim, LANES), 1)
    picks = []
    for side in range(2):
        wanted = down_columns(send[side : side + 1, :])
        picks.append(
            jnp.concatenate(
                [as_bf16(wanted == lane + t * LANES) for t in range(slots // LANES)], axis=1
            )
        )
    pick = jnp.concatenate(picks, axis=0)

    loads[3].wait()
    listed = entries[...]
    from_left = (listed >= slots) & (listed < slots + rim)
    from_right = listed >= slots + rim
    listed = jnp.where(from_left & (n == 0), -1, listed)
    entries[...] = jnp.where(from_right & (n == columns - 1), -1, listed)
    slot_lane = iota((slots, LANES), 1)

    def build(k):
        wanted = down_columns(entries[k : k + 1, :])
        for t in range(hot.shape[2] // LANES):
            hot[k, :, t * LANES : (t + 1) * LANES] = as_bf16(wanted == slot_lane + t * LANES)

    sides = ((1, has_before, 0, before_in), (0, has_after, 4, after_in))

    def hear_columns():
        for _, has, listener, semaphore in sides:

            @pl.when((g == listener) & has)
            def _():
                pl.semaphore_wait(barrier, groups)
                for member in range(groups):
                    if member != listener:
                        tell(semaphore, member, n)

    def know_column(has, listener, semaphore):
        @pl.when((g != listener) & has)
        def _():
            pl.semaphore_wait(semaphore, 1)

    def pass_on(c):
        for d in range(1, groups):
            relay(c, d).wait_recv()
        offer[c] = nn_dot(pick, own[c]).astype(BF16)
        for side, has, listener, semaphore in sides:
            if c == 0:
                know_column(has, listener, semaphore)

            @pl.when(has)
            def _():
                hand(c, side).start()

    def half_of(ref, h):
        return jnp.concatenate([ref[per * h + i] for i in range(per)], axis=1)

    def from_own(h):
        local = half_of(own, h)
        for k in range(offsets):
            cols[h, k] = nn_dot(hot[k, :, :slots], local).astype(BF16)

    @pl.when((g == 2) & apart)
    def _():
        pl.semaphore_wait(barrier, groups - 2)
        for member in range(1, groups):
            if member != 2:
                tell(group_in, member, n)

    @pl.when((g != 0) & (g != 4) & (n > 0))
    def _():
        pl.semaphore_wait(barrier, groups - 1)

    @pl.when(((g == 1) | (g == 5)) & (n > 0))
    def _():
        tell(group_in, g - 1, n)

    @pl.when(((g == 0) | (g == 4)) & (n > 0))
    def _():
        pl.semaphore_wait(group_in, 1)

    @pl.when(((g == 1) | (g > 2)) & apart)
    def _():
        pl.semaphore_wait(group_in, 1)

    for c in range(chunks):
        for d in range(1, groups):

            @pl.when((n > 0) | ((g > 0) & (g + d != groups)))
            def _():
                relay(c, d).start()

    @pl.when((g == 0) & apart)
    def _():
        pl.semaphore_wait(first_in, 1)
        for c in range(chunks):
            for d in range(1, groups):
                relay(c, d).start()

    for k in range(offsets):
        build(k)

    for i in (4, 5, 6):
        loads[i].wait()
    blocks[...] = jnp.zeros(blocks.shape, BF16)
    for q in range(octants):
        blocks[q, pl.ds(q * parents, parents), :] = par[...]
    translated = nt_dot(l2l[0], blocks[0])
    for q in range(1, octants):
        translated = translated + nt_dot(l2l[q], blocks[q])
    upper = translated.astype(BF16)
    lower = (translated - upper.astype(F32)).astype(BF16)
    child = as_bf16(iota((octants * parents, slots), 0) == pof[...])
    out_ref[...] = nn_dot(upper, child) + nn_dot(lower, child)
    @pl.when((g == 1) & apart)
    def _():
        pl.semaphore_wait(barrier, 1)
        for member in range(groups):
            if member != 1:
                tell(first_in, member, n)

    @pl.when((g > 1) & apart)
    def _():
        pl.semaphore_wait(first_in, 1)

    @pl.when((g > 0) & apart)
    def _():
        for c in range(chunks):
            relay(c, groups - g).start()

    hear_columns()
    for c in range(chunks):
        pass_on(c)
    for h in range(halves):
        from_own(h)

    @pl.when(n == 0)
    def _():
        near[:, :rim] = jnp.zeros((chunks, rim, WIDTH), BF16)

    @pl.when(n == columns - 1)
    def _():
        near[:, rim:] = jnp.zeros((chunks, rim, WIDTH), BF16)

    loads[7].wait()
    for h in range(halves):
        for c in range(per * h, per * h + per):
            for side, has in enumerate((has_before, has_after)):

                @pl.when(has)
                def _():
                    hand(c, side).wait_recv()

        beside = half_of(near, h)
        for k in range(offsets):
            cols[h, k] = cols[h, k] + nn_dot(hot[k, :, slots:], beside).astype(BF16)
        first = h * HALF
        width = min(HALF, coef - first)
        total = out_ref[...]
        for k in range(offsets):
            total = total + nt_dot(m2l[k, :, first : first + width], cols[h, k, :, :width])
        out_ref[...] = total

    for c in range(chunks):
        for d in range(1, groups):
            relay(c, d).wait_send()
        for side, has in enumerate((has_after, has_before)):

            @pl.when(has)
            def _():
                hand(c, side).wait_send()


def body(multipole, dest, parent_local, parent_of, send_list, lists, m2l_ops, l2l_ops):
    groups, columns = lax.axis_size("grp"), lax.axis_size("nbr")
    coef, boxes = multipole.shape
    offsets, slots = lists.shape
    octants = l2l_ops.shape[0]
    rim = send_list.shape[1]
    parents = parent_local.shape[1]
    chunks = -(-coef // HALF) * (HALF // WIDTH)
    dest_row = dest.reshape(1, boxes)
    parent_rows = parent_local.T
    child_row = parent_of.reshape(1, slots)
    args = [
        pltpu.with_memory_space_constraint(a, pltpu.HBM)
        for a in (multipole, dest_row, parent_rows, child_row, send_list, lists, m2l_ops, l2l_ops)
    ]
    return pl.pallas_call(
        functools.partial(
            kernel, groups, columns, coef, boxes, slots, rim, parents, offsets, octants, chunks
        ),
        out_shape=jax.ShapeDtypeStruct((coef, slots), F32),
        in_specs=[pl.BlockSpec(memory_space=pltpu.HBM)] * len(args),
        out_specs=pl.BlockSpec(memory_space=pltpu.VMEM),
        scratch_shapes=[pltpu.VMEM(a.shape, a.dtype) for a in args]
        + [
            pltpu.VMEM((chunks, slots, WIDTH), BF16),
            pltpu.VMEM((chunks, slots, WIDTH), BF16),
            pltpu.VMEM((chunks, 2 * rim, WIDTH), BF16),
            pltpu.VMEM((chunks, 2 * rim, WIDTH), BF16),
            pltpu.VMEM((offsets, slots, slots + 2 * rim), BF16),
            pltpu.VMEM((-(-coef // HALF), offsets, slots, HALF), BF16),
            pltpu.VMEM((octants, octants * parents, coef), BF16),
            pltpu.SemaphoreType.DMA((len(args),)),
            pltpu.SemaphoreType.DMA((chunks, groups - 1)),
            pltpu.SemaphoreType.DMA((chunks, groups - 1)),
            pltpu.SemaphoreType.DMA((chunks, 2)),
            pltpu.SemaphoreType.DMA((chunks, 2)),
            pltpu.SemaphoreType.REGULAR,
            pltpu.SemaphoreType.REGULAR,
            pltpu.SemaphoreType.REGULAR,
            pltpu.SemaphoreType.REGULAR,
        ],
        compiler_params=pltpu.CompilerParams(
            collective_id=0, has_side_effects=True, vmem_limit_bytes=48 * 1024 * 1024
        ),
        name="downward",
    )(*args)


def solution(mesh):
    placed = (
        P(None, ("grp", "nbr")),
        P(("grp", "nbr"), None),
        P(None, ("grp", "nbr")),
        P(("grp", "nbr")),
        P(None, ("grp", "nbr")),
        P(None, ("grp", "nbr")),
        P(),
        P(),
    )
    return jax.shard_map(
        body, mesh=mesh, in_specs=placed, out_specs=P(None, ("grp", "nbr")), check_vma=False
    )
```
